32 devices in a mesh: groups: 2 (over x), ep: 16 (over z, y, core).
Axes of the slice: x: 2, y: 2, z: 4, core: 2. Of those that a mesh axis runs over, the one named last changes fastest.
Arguments:
- rows_in: bfloat16 [4096, 7168], P(('groups', 'ep')), parts along dimension 0, may hold values from -6 to 6
- expert_ids: int32 [4096, 8], P(('groups', 'ep')), parts along dimension 0, may hold values from 0 to 255, all different within a row; in each aligned block of 128 rows (0 to 127, 128 to 255, ...) at most 8 rows name the same one
- gate_values: float32 [4096, 8], P(('groups', 'ep')), parts along dimension 0, may hold values from 0.2 to 1
- gate_w: bfloat16 [7168, 8192], P(None, 'ep'), may hold values from -0.0625 to 0.0625
- up_w: bfloat16 [7168, 8192], P(None, 'ep'), may hold values from -0.0625 to 0.0625
- down_w: bfloat16 [8192, 7168], P('ep'), may hold values from -0.125 to 0.125
Outputs:
- mixed: bfloat16 [4096, 7168], P(('groups', 'ep')), parts along dimension 0
The draws below stay inside these ranges and needn't reach their ends.
There are 2 independent parts, one for each index of `groups`. The reference program is written for one: setup_inputs(seed, part) draws one part's arguments, and reference() takes and returns one part's arrays. A program takes and returns all parts, laid end to end along the dimension named above; an argument that names none is the same for every part. Nothing has to cross between parts.
Inputs may be any that keep to these rules, and one draw needn't show every extreme that they name: `expert_ids`: each row names 8 different experts. Among the rows of one device no expert is named more than 8 times.
All inputs are finite; a program needn't handle non-finite values.
Results may differ from the reference program's by a relative error of at most 0.0049.
Values may be sent and summed in bfloat16 or wider, within the bound.
A program may use at most 128 MiB of HBM per device.

```python
import math
import jax
import jax.numpy as jnp
import numpy as np
from jax import lax

D = 7168
FF = 2048
NEXP = 256
TOPK = 8
ETP = 4
R_DEV = 128
CAP = 8
WIN = 4
ROWS = 2048
N_EP = 16


def levels(rng, dims, cuts, low, high):
    factor_of, own = 1.0, jax.random.fold_in(rng, 6)
    for dim, blocks in cuts:
        heights = jnp.exp(jax.random.uniform(jax.random.fold_in(own, dim), (blocks,), jnp.float32, low / len(cuts), high / len(cuts)))
        factor_of = factor_of * jnp.repeat(heights, dims[dim] // blocks).reshape([-1 if axis == dim else 1 for axis in range(len(dims))])
    return factor_of


def assign_block(stream_key, own, number, rows, amount, top, reach, lean):
    order = jax.random.permutation(stream_key, amount)
    packed, ordinary = portions_of(amount, rows * top, reach, lean, True), portions_of(amount, rows * top, reach, lean, False)
    places = jnp.arange(amount)

    def named(tallies, offset_by):
        used = int((tallies > 0).sum())
        fixed = max(1, used // 4)
        passed = fixed + (places - fixed + offset_by * (used - fixed)) % max(1, amount - fixed)
        return jnp.zeros((amount,), jnp.int32).at[order[jnp.where(places < fixed, places, passed)]].set(jnp.asarray(tallies, jnp.int32))

    tallies = jnp.where(number % 4 == 0, named(packed, number // 4), named(ordinary, number - number // 4 - 1))
    mixed = jax.random.permutation(jax.random.fold_in(own, 3), amount)
    giver, taker = mixed[0:amount // 2 * 2:2], mixed[1:amount // 2 * 2:2]
    room = jnp.minimum(tallies[giver] - 1, reach - tallies[taker]) // 2
    room = jnp.where((giver == order[0]) | (taker == order[0]) | (tallies[taker] == 0), 0, jnp.maximum(room, 0))
    passed = jax.random.randint(jax.random.fold_in(own, 4), (amount // 2,), 0, 1 << 20) % (room + 1)
    tallies = tallies.at[giver].add(-passed).at[taker].add(passed)
    members = jnp.searchsorted(jnp.cumsum(tallies), jnp.arange(rows * top), side="right").astype(jnp.int32)
    grid = members.reshape(top, rows).T
    grid = grid[jax.random.permutation(jax.random.fold_in(own, 1), rows)]
    offset_by = jax.random.randint(jax.random.fold_in(own, 2), (rows, 1), 0, top)
    return jnp.take_along_axis(grid, (jnp.arange(top)[None, :] + offset_by) % top, axis=1)


def portions_of(number_of, total, most, slope, full):
    weights = [(1 << 20) // math.isqrt(standing ** slope) + 1 for standing in range(1, number_of + 1)]
    largest = most if full else min(most, max(-(-total // number_of), total * weights[0] // sum(weights)))
    least = 1 if total - largest >= number_of - 1 else 0
    holding, rest = [largest] + [least] * (number_of - 1), total - largest - least * (number_of - 1)
    while rest > 0:
        free = [i for i in range(1, number_of) if holding[i] < largest] or [i for i in range(1, number_of) if holding[i] < most]
        mass, left = sum([weights[i] for i in free]), rest
        for i in free:
            addition = min(most - holding[i], max(1, left * weights[i] // mass), rest)
            holding[i] = holding[i] + addition
            rest = rest - addition
    return np.array(holding)


def gaussian(own_key, extent, spread, limit, split=(), kind=jnp.bfloat16):
    gain = levels(own_key, extent, split, -0.22, 0.18) if split else 1.0
    drawn = jax.random.normal(own_key, extent, jnp.float32) * spread * gain
    return jnp.minimum(jnp.maximum(drawn, -limit), limit).astype(kind)


def setup_inputs(seed: int = 0, part: int = 0) -> dict:
    streams_of = jax.random.split(jax.random.key(seed), 7)
    part_keys = jax.random.split(jax.random.fold_in(streams_of[6], part), 7)
    rows_in = gaussian(part_keys[0], (ROWS, D), 1.0, 6.0, ((0, 16),))
    expert_ids_keys = jax.random.split(jax.random.fold_in(part_keys[1], 1), ROWS // R_DEV)
    expert_ids_turns = jax.random.permutation(jax.random.fold_in(part_keys[1], 3), ROWS // R_DEV)
    expert_ids = jax.vmap(lambda own, number: assign_block(jax.random.fold_in(part_keys[1], 2), own, number, R_DEV, NEXP, TOPK, CAP, 2))(expert_ids_keys, expert_ids_turns).reshape((ROWS, TOPK))
    gate_values = jnp.clip(0.2 + 0.8 * jax.random.uniform(part_keys[2], (ROWS, TOPK), jnp.float32) ** levels(part_keys[2], (ROWS, TOPK), ((0, 16),), -0.2, 0.2), 0.2, 1.0)
    gate_w = gaussian(streams_of[3], (D, WIN * FF), D ** -0.5, 0.0625, ((1, 16),))
    up_w = gaussian(streams_of[4], (D, WIN * FF), D ** -0.5, 0.0625, ((1, 16),))
    down_w = gaussian(streams_of[5], (WIN * FF, D), FF ** -0.5, 0.125, ((0, 16),))
    return {"rows_in": rows_in, "expert_ids": expert_ids, "gate_values": gate_values, "gate_w": gate_w, "up_w": up_w, "down_w": down_w}


def tables(ids_block, gates_block, window):
    flat = ids_block.reshape(-1)
    onehot = (flat[:, None] == jnp.arange(window, dtype=jnp.int32)[None, :]).astype(jnp.int32)
    before = jnp.cumsum(onehot, axis=0) - onehot
    place = jnp.sum(before * onehot, axis=1)
    target = jnp.where(flat < window, flat * CAP + place, -1).reshape(ids_block.shape)
    match = target[:, :, None] == jnp.arange(window * CAP, dtype=jnp.int32)[None, None, :]
    picker = jnp.sum(match.astype(jnp.float32), axis=1)
    weights = jnp.sum(jnp.where(match, gates_block[:, :, None], jnp.float32(0.0)), axis=1)
    return picker, weights


def reference(rows_in, expert_ids, gate_values, gate_w, up_w, down_w):
    window = N_EP // ETP
    blocks = rows_in.reshape(N_EP, R_DEV, D)
    picker, weights = jax.vmap(lambda a, b: tables(a, b, window))(expert_ids.reshape(N_EP, R_DEV, TOPK), gate_values.reshape(N_EP, R_DEV, TOPK))
    buffer = jnp.einsum("nrs,nrd->nsd", picker, blocks.astype(jnp.float32)).astype(jnp.bfloat16)
    grouped = buffer.reshape(N_EP, window, CAP, D).transpose(1, 0, 2, 3).reshape(window, N_EP * CAP, D)

    def expert(number):
        start = (number * FF).astype(jnp.int32)
        inputs = lax.dynamic_index_in_dim(grouped, number, 0, keepdims=False)
        gate = jnp.dot(inputs, lax.dynamic_slice_in_dim(gate_w, start, FF, 1), preferred_element_type=jnp.float32)
        upper = jnp.dot(inputs, lax.dynamic_slice_in_dim(up_w, start, FF, 1), preferred_element_type=jnp.float32)
        hidden = (jax.nn.silu(gate) * upper).astype(jnp.bfloat16)
        return jnp.dot(hidden, lax.dynamic_slice_in_dim(down_w, start, FF, 0), preferred_element_type=jnp.float32)

    outputs = lax.map(expert, jnp.arange(window, dtype=jnp.int32))
    outputs = outputs.reshape(window, N_EP, CAP, D).transpose(1, 0, 2, 3).reshape(N_EP, window * CAP, D)
    mixed = jnp.einsum("nrs,nsd->nrd", weights, outputs, precision=lax.Precision.HIGHEST)
    return mixed.reshape(N_EP * R_DEV, D).astype(jnp.bfloat16)
```

```python
import functools

import jax
import jax.numpy as jnp
from jax import lax
from jax.experimental import pallas as pl
from jax.experimental.pallas import tpu as pltpu
from jax.sharding import PartitionSpec as P

ETP = 4
CAP = 8
MESH = pl.DeviceIdType.MESH


def flip(number, mask):
    result = number
    bit = 1
    while bit <= mask:
        if mask & bit:
            digit = lax.rem(lax.div(number, jnp.int32(bit)), jnp.int32(2))
            result = result + bit - 2 * bit * digit
        bit *= 2
    return result


def kernel(
    window, chunks,
    ids_ref, gates_ref, rows_hbm, gate_hbm, up_hbm, down_hbm,
    out_ref,
    rows, gate_w, up_w, down_w, block, arrived, inputs, hidden,
    own, core_out, core_in, side_out, side_in, home_out, home_in,
    load_sem, disp_send, disp_recv, core_send, core_recv, side_send, side_recv,
    home_send, home_recv,
):
    width = rows.shape[1]
    row_count = rows.shape[0]
    piece = width // chunks
    slots = window * CAP
    me = lax.axis_index("ep")
    plane = lax.div(me, jnp.int32(ETP))
    within = lax.rem(me, jnp.int32(ETP))
    sibling = plane * ETP + flip(within, 1)
    side = plane * ETP + flip(within, 2)
    partner = [flip(plane, d) * ETP + within for d in range(window)]

    loads = [
        pltpu.make_async_copy(src, dst, load_sem.at[i])
        for i, (src, dst) in enumerate(
            ((rows_hbm, rows), (gate_hbm, gate_w), (up_hbm, up_w), (down_hbm, down_w))
        )
    ]
    loads[0].start()

    barrier = pltpu.get_barrier_semaphore()
    peers = partner[1:] + [sibling, side]
    for peer in peers:
        pl.semaphore_signal(barrier, inc=1, device_id={"ep": peer}, device_id_type=MESH)

    def remote(src, dst, send, recv, target):
        return pltpu.make_async_remote_copy(
            src_ref=src, dst_ref=dst, send_sem=send, recv_sem=recv,
            device_id={"ep": target}, device_id_type=MESH,
        )

    ids = ids_ref[...]
    gates = gates_ref[...]
    named, valued = [], []
    for d in range(window):
        hit = ids == flip(plane, d)
        one = jnp.sum(jnp.where(hit, 1.0, 0.0), axis=0, keepdims=True)
        val = jnp.sum(jnp.where(hit, gates, 0.0), axis=0, keepdims=True)
        named.append(jnp.broadcast_to(one, (CAP, row_count)))
        valued.append(jnp.broadcast_to(val, (CAP, row_count)))
    named = jnp.concatenate(named, axis=0)
    valued = jnp.concatenate(valued, axis=0)
    earlier = lax.broadcasted_iota(jnp.int32, (row_count, row_count), 0) < lax.broadcasted_iota(
        jnp.int32, (row_count, row_count), 1
    )
    rank = jnp.dot(
        named.astype(jnp.bfloat16),
        jnp.where(earlier, 1.0, 0.0).astype(jnp.bfloat16),
        preferred_element_type=jnp.float32,
    )
    place = lax.rem(lax.broadcasted_iota(jnp.int32, (slots, row_count), 0), jnp.int32(CAP))
    chosen = jnp.logical_and(rank == place.astype(jnp.float32), named > 0.5)
    picker = jnp.where(chosen, 1.0, 0.0).astype(jnp.bfloat16)
    weights = jnp.where(chosen, valued, 0.0)
    high = weights.astype(jnp.bfloat16)
    low = (weights - high.astype(jnp.float32)).astype(jnp.bfloat16)
    both = jnp.concatenate([high.astype(jnp.float32), low.astype(jnp.float32)], axis=0)
    both = jnp.transpose(both).astype(jnp.bfloat16)

    loads[0].wait()
    for load in loads[1:]:
        load.start()
    for k in range(chunks):
        cols = pl.ds(k * piece, piece)
        part = jnp.dot(picker, rows[:, cols], preferred_element_type=jnp.float32)
        part = part.reshape(window, CAP, piece).astype(jnp.bfloat16)
        arrived[0, 0, :, cols] = part[0]
        for d in range(1, window):
            block[d, :, cols] = part[d]

    pl.semaphore_wait(barrier, len(peers))
    along, core, across, relay = [None], [], [], []
    for d in range(window):
        if d:
            along.append(
                remote(block.at[d], arrived.at[0, d], disp_send.at[0, d], disp_recv.at[0, d], partner[d])
            )
        core.append(
            remote(arrived.at[0, d], arrived.at[1, d], disp_send.at[1, d], disp_recv.at[1, d], sibling)
        )
        across.append(
            remote(arrived.at[0, d], arrived.at[2, d], disp_send.at[2, d], disp_recv.at[2, d], side)
        )
        relay.append(
            remote(arrived.at[2, d], arrived.at[3, d], disp_send.at[3, d], disp_recv.at[3, d], sibling)
        )
    across[0].start()
    for d in range(1, window):
        along[d].start()
    core[0].start()
    for d in range(1, window):
        along[d].wait_recv()
        across[d].start()
        core[d].start()
        across[d - 1].wait_recv()
        relay[d - 1].start()

    def gather(g):
        values = arrived[g].astype(jnp.float32).reshape(slots, width)
        inputs[g * slots:(g + 1) * slots, :] = values.astype(jnp.bfloat16)

    gather(0)
    for d in range(window):
        core[d].wait_recv()
    gather(1)
    across[window - 1].wait_recv()
    relay[window - 1].start()
    gather(2)
    for d in range(window):
        relay[d].wait_recv()
    gather(3)

    loads[1].wait()
    loads[2].wait()
    units = gate_w.shape[1]
    tile = 256

    @pl.loop(0, units // tile)
    def _(n):
        cols = pl.ds(pl.multiple_of(n * tile, tile), tile)
        g = jnp.dot(inputs[...], gate_w[:, cols], preferred_element_type=jnp.float32)
        u = jnp.dot(inputs[...], up_w[:, cols], preferred_element_type=jnp.float32)
        hidden[:, cols] = (g / (1.0 + jnp.exp(-g)) * u).astype(jnp.bfloat16)

    loads[3].wait()
    to_core = [
        remote(core_out.at[k], core_in.at[k], core_send.at[k], core_recv.at[k], sibling)
        for k in range(chunks)
    ]
    to_side = [
        remote(side_out.at[k], side_in.at[k], side_send.at[k], side_recv.at[k], side)
        for k in range(chunks)
    ]
    to_home = [
        [
            remote(home_out.at[k, d], home_in.at[k, d], home_send.at[k, d], home_recv.at[k, d], partner[d])
            for d in range(1, window)
        ]
        for k in range(chunks)
    ]

    def pair_sum(k):
        to_core[k].wait_recv()
        side_out[k] = (own[k, slots:, :] + core_in[k, slots:, :].astype(jnp.float32)).astype(jnp.bfloat16)
        to_side[k].start()
        own[k, :slots, :] = own[k, :slots, :] + core_in[k, :slots, :].astype(jnp.float32)

    def full_sum(k):
        to_side[k].wait_recv()
        total = own[k, :slots, :] + side_in[k].astype(jnp.float32)
        total = total.reshape(window, CAP, piece).astype(jnp.bfloat16)
        home_in[k, 0] = total[0]
        for d in range(1, window):
            home_out[k, d] = total[d]
        for copy in to_home[k]:
            copy.start()

    def mix(k):
        for copy in to_home[k]:
            copy.wait_recv()
        values = home_in[k].astype(jnp.float32).reshape(slots, piece)
        values = jnp.concatenate([values, values], axis=0).astype(jnp.bfloat16)
        out_ref[:, k * piece:(k + 1) * piece] = jnp.dot(
            both, values, preferred_element_type=jnp.float32
        ).astype(jnp.bfloat16)

    for k in range(chunks):
        part = jnp.dot(
            hidden[...], down_w[:, k * piece:(k + 1) * piece], preferred_element_type=jnp.float32
        )
        core_out[k, :slots, :] = part[slots:2 * slots].astype(jnp.bfloat16)
        core_out[k, slots:, :] = part[3 * slots:].astype(jnp.bfloat16)
        to_core[k].start()
        own[k, :slots, :] = part[:slots]
        own[k, slots:, :] = part[2 * slots:3 * slots]
        if k >= 1:
            pair_sum(k - 1)
    pair_sum(chunks - 1)
    for k in range(chunks):
        full_sum(k)
        if k >= 2:
            mix(k - 2)
    for k in range(max(chunks - 2, 0), chunks):
        mix(k)

    for copy in along[1:] + core + across + relay + to_core + to_side:
        copy.wait_send()
    for k in range(chunks):
        for copy in to_home[k]:
            copy.wait_send()


def body(rows_in, expert_ids, gate_values, gate_w, up_w, down_w):
    devices = lax.axis_size("ep")
    row_count, width = rows_in.shape
    units = gate_w.shape[1]
    window = devices // ETP
    slots = window * CAP
    chunks = 7
    piece = width // chunks
    bf16, f32 = jnp.bfloat16, jnp.float32
    dma = pltpu.SemaphoreType.DMA
    any_spec = pl.BlockSpec(memory_space=pl.ANY)
    vmem_spec = pl.BlockSpec(memory_space=pltpu.VMEM)
    return pl.pallas_call(
        functools.partial(kernel, window, chunks),
        out_shape=jax.ShapeDtypeStruct((row_count, width), bf16),
        in_specs=[vmem_spec, vmem_spec, any_spec, any_spec, any_spec, any_spec],
        out_specs=vmem_spec,
        scratch_shapes=[
            pltpu.VMEM((row_count, width), bf16),
            pltpu.VMEM((width, units), bf16),
            pltpu.VMEM((width, units), bf16),
            pltpu.VMEM((units, width), bf16),
            pltpu.VMEM((window, CAP, width), bf16),
            pltpu.VMEM((ETP, window, CAP, width), bf16),
            pltpu.VMEM((ETP * slots, width), bf16),
            pltpu.VMEM((ETP * slots, units), bf16),
            pltpu.VMEM((chunks, 2 * slots, piece), f32),
            pltpu.VMEM((chunks, 2 * slots, piece), bf16),
            pltpu.VMEM((chunks, 2 * slots, piece), bf16),
            pltpu.VMEM((chunks, slots, piece), bf16),
            pltpu.VMEM((chunks, slots, piece), bf16),
            pltpu.VMEM((chunks, window, CAP, piece), bf16),
            pltpu.VMEM((chunks, window, CAP, piece), bf16),
            dma((4,)),
            dma((4, window)),
            dma((4, window)),
            dma((chunks,)),
            dma((chunks,)),
            dma((chunks,)),
            dma((chunks,)),
            dma((chunks, window)),
            dma((chunks, window)),
        ],
        compiler_params=pltpu.CompilerParams(
            collective_id=0, has_side_effects=True, vmem_limit_bytes=56 * 1024 * 1024
        ),
    )(expert_ids.T, gate_values.T, rows_in, gate_w, up_w, down_w)


def solution(mesh):
    in_specs = (
        P(("groups", "ep"), None),
        P(("groups", "ep"), None),
        P(("groups", "ep"), None),
        P(None, "ep"),
        P(None, "ep"),
        P("ep", None),
    )
    out_specs = P(("groups", "ep"), None)
    return jax.shard_map(body, mesh=mesh, in_specs=in_specs, out_specs=out_specs, check_vma=False)
```

```python
import functools

import jax
import jax.numpy as jnp
from jax import lax
from jax.experimental import pallas as pl
from jax.experimental.pallas import tpu as pltpu
from jax.sharding import PartitionSpec as P

ETP = 4
CAP = 8
MESH = pl.DeviceIdType.MESH


def flip(number, mask):
    result = number
    bit = 1
    while bit <= mask:
        if mask & bit:
            digit = lax.rem(lax.div(number, jnp.int32(bit)), jnp.int32(2))
            result = result + bit - 2 * bit * digit
        bit *= 2
    return result


def kernel(
    window, chunks, halves,
    ids_ref, gates_ref, rows_hbm, gate_hbm, up_hbm, down_hbm,
    mix_ref, out_ref,
    rows, gate_w, up_w, down_w, block, arrived, inputs, gate_sum, up_sum, hidden,
    own, core_out, core_in, side_out, side_in, home_out, home_in,
    load_sem, disp_send, disp_recv, core_send, core_recv, side_send, side_recv,
    home_send, home_recv,
):
    width = rows.shape[1]
    row_count = rows.shape[0]
    piece = width // chunks
    slots = window * CAP
    me = lax.axis_index("ep")
    plane = lax.div(me, jnp.int32(ETP))
    within = lax.rem(me, jnp.int32(ETP))
    sibling = plane * ETP + flip(within, 1)
    side = plane * ETP + flip(within, 2)
    partner = [flip(plane, d) * ETP + within for d in range(window)]

    loads = [
        pltpu.make_async_copy(src, dst, load_sem.at[i])
        for i, (src, dst) in enumerate(
            ((rows_hbm, rows), (gate_hbm, gate_w), (up_hbm, up_w), (down_hbm, down_w))
        )
    ]
    loads[0].start()

    barrier = pltpu.get_barrier_semaphore()
    peers = partner[1:] + [sibling, side]
    for peer in peers:
        pl.semaphore_signal(barrier, inc=1, device_id={"ep": peer}, device_id_type=MESH)

    def remote(src, dst, send, recv, target):
        return pltpu.make_async_remote_copy(
            src_ref=src, dst_ref=dst, send_sem=send, recv_sem=recv,
            device_id={"ep": target}, device_id_type=MESH,
        )

    ids = ids_ref[...]
    gates = gates_ref[...]
    named, valued = [], []
    for d in range(window):
        hit = ids == flip(plane, d)
        one = jnp.sum(jnp.where(hit, 1.0, 0.0), axis=0, keepdims=True)
        val = jnp.sum(jnp.where(hit, gates, 0.0), axis=0, keepdims=True)
        named.append(jnp.broadcast_to(one, (CAP, row_count)))
        valued.append(jnp.broadcast_to(val, (CAP, row_count)))
    named = jnp.concatenate(named, axis=0)
    valued = jnp.concatenate(valued, axis=0)
    earlier = lax.broadcasted_iota(jnp.int32, (row_count, row_count), 0) < lax.broadcasted_iota(
        jnp.int32, (row_count, row_count), 1
    )
    rank = jnp.dot(
        named.astype(jnp.bfloat16),
        jnp.where(earlier, 1.0, 0.0).astype(jnp.bfloat16),
        preferred_element_type=jnp.float32,
    )
    place = lax.rem(lax.broadcasted_iota(jnp.int32, (slots, row_count), 0), jnp.int32(CAP))
    chosen = jnp.logical_and(rank == place.astype(jnp.float32), named > 0.5)
    picker = jnp.where(chosen, 1.0, 0.0).astype(jnp.bfloat16)
    weights = jnp.where(chosen, valued, 0.0)
    high = weights.astype(jnp.bfloat16)
    low = (weights - high.astype(jnp.float32)).astype(jnp.bfloat16)
    both = jnp.concatenate([high.astype(jnp.float32), low.astype(jnp.float32)], axis=0)
    mix_ref[...] = jnp.transpose(both).astype(jnp.bfloat16)

    half = width // halves
    along, core, across, relay = [], [], [], []
    for h in range(halves):
        for d in range(window):
            n = h * window + d
            along.append(
                remote(block.at[h, d], arrived.at[h, 0, d], disp_send.at[0, n], disp_recv.at[0, n], partner[d])
                if d else None
            )
            core.append(
                remote(arrived.at[h, 0, d], arrived.at[h, 1, d], disp_send.at[1, n], disp_recv.at[1, n], sibling)
            )
            across.append(
                remote(arrived.at[h, 0, d], arrived.at[h, 2, d], disp_send.at[2, n], disp_recv.at[2, n], side)
            )
            relay.append(
                remote(arrived.at[h, 2, d], arrived.at[h, 3, d], disp_send.at[3, n], disp_recv.at[3, n], sibling)
            )

    loads[0].wait()
    for h in range(halves):
        part = jnp.dot(
            picker, rows[:, h * half:(h + 1) * half], preferred_element_type=jnp.float32
        )
        part = part.reshape(window, CAP, half).astype(jnp.bfloat16)
        arrived[h, 0, 0] = part[0]
        for d in range(1, window):
            block[h, d] = part[d]
        if h == 0:
            pl.semaphore_wait(barrier, len(peers))
        across[h * window].start()
        for d in range(1, window):
            along[h * window + d].start()
        core[h * window].start()
    for load in loads[1:]:
        load.start()

    passed = 0
    for h in range(halves):
        for d in range(1, window):
            n = h * window + d
            along[n].wait_recv()
            across[n].start()
            core[n].start()
            while passed < n and (passed + 1 < n or d > 1):
                across[passed].wait_recv()
                relay[passed].start()
                passed += 1

    def gather(h, g):
        values = arrived[h, g].astype(jnp.float32).reshape(slots, half)
        inputs[h, g * slots:(g + 1) * slots, :] = values.astype(jnp.bfloat16)

    units = gate_w.shape[1]
    tile = 256
    for h in range(halves):
        last = h == halves - 1
        gather(h, 0)
        for d in range(window):
            core[h * window + d].wait_recv()
        gather(h, 1)
        while passed < (h + 1) * window:
            across[passed].wait_recv()
            relay[passed].start()
            passed += 1
        gather(h, 2)
        for d in range(window):
            relay[h * window + d].wait_recv()
        gather(h, 3)
        if h == 0:
            loads[1].wait()
            loads[2].wait()

        @pl.loop(0, units // tile)
        def _(n):
            cols = pl.ds(pl.multiple_of(n * tile, tile), tile)
            deep = pl.ds(h * half, half)
            g = jnp.dot(inputs[h], gate_w[deep, cols], preferred_element_type=jnp.float32)
            u = jnp.dot(inputs[h], up_w[deep, cols], preferred_element_type=jnp.float32)
            if h > 0:
                g = g + gate_sum[:, cols]
                u = u + up_sum[:, cols]
            if last:
                hidden[:, cols] = (g / (1.0 + jnp.exp(-g)) * u).astype(jnp.bfloat16)
            else:
                gate_sum[:, cols] = g
                up_sum[:, cols] = u

    loads[3].wait()
    to_core = [
        remote(core_out.at[k], core_in.at[k], core_send.at[k], core_recv.at[k], sibling)
        for k in range(chunks)
    ]
    to_side = [
        remote(side_out.at[k], side_in.at[k], side_send.at[k], side_recv.at[k], side)
        for k in range(chunks)
    ]
    to_home = [
        [
            remote(home_out.at[k, d], home_in.at[k, d], home_send.at[k, d], home_recv.at[k, d], partner[d])
            for d in range(1, window)
        ]
        for k in range(chunks)
    ]

    def pair_sum(k):
        to_core[k].wait_recv()
        side_out[k] = (own[k, slots:, :] + core_in[k, slots:, :].astype(jnp.float32)).astype(jnp.bfloat16)
        to_side[k].start()
        own[k, :slots, :] = own[k, :slots, :] + core_in[k, :slots, :].astype(jnp.float32)

    def full_sum(k):
        to_side[k].wait_recv()
        total = own[k, :slots, :] + side_in[k].astype(jnp.float32)
        total = total.reshape(window, CAP, piece).astype(jnp.bfloat16)
        home_in[k, 0] = total[0]
        for d in range(1, window):
            home_out[k, d] = total[d]
        for copy in to_home[k]:
            copy.start()

    def mix(k):
        for copy in to_home[k]:
            copy.wait_recv()
        values = home_in[k].astype(jnp.float32).reshape(slots, piece)
        values = values.astype(jnp.bfloat16)
        out_ref[:slots, k * piece:(k + 1) * piece] = values
        out_ref[slots:, k * piece:(k + 1) * piece] = values

    for k in range(chunks):
        part = jnp.dot(
            hidden[...], down_w[:, k * piece:(k + 1) * piece], preferred_element_type=jnp.float32
        )
        core_out[k, :slots, :] = part[slots:2 * slots].astype(jnp.bfloat16)
        core_out[k, slots:, :] = part[3 * slots:].astype(jnp.bfloat16)
        to_core[k].start()
        own[k, :slots, :] = part[:slots]
        own[k, slots:, :] = part[2 * slots:3 * slots]
        if k >= 1:
            pair_sum(k - 1)
    pair_sum(chunks - 1)
    for k in range(chunks):
        full_sum(k)
    for k in range(chunks):
        mix(k)

    sent = [copy for copy in along if copy is not None]
    for copy in sent + core + across + relay + to_core + to_side:
        copy.wait_send()
    for k in range(chunks):
        for copy in to_home[k]:
            copy.wait_send()


def body(rows_in, expert_ids, gate_values, gate_w, up_w, down_w):
    devices = lax.axis_size("ep")
    row_count, width = rows_in.shape
    units = gate_w.shape[1]
    window = devices // ETP
    slots = window * CAP
    chunks = 7
    halves = 2
    half = width // halves
    piece = width // chunks
    bf16, f32 = jnp.bfloat16, jnp.float32
    dma = pltpu.SemaphoreType.DMA
    any_spec = pl.BlockSpec(memory_space=pl.ANY)
    vmem_spec = pl.BlockSpec(memory_space=pltpu.VMEM)
    mix, values = pl.pallas_call(
        functools.partial(kernel, window, chunks, halves),
        out_shape=(
            jax.ShapeDtypeStruct((row_count, 2 * slots), bf16),
            jax.ShapeDtypeStruct((2 * slots, width), bf16),
        ),
        in_specs=[vmem_spec, vmem_spec, any_spec, any_spec, any_spec, any_spec],
        out_specs=(vmem_spec, vmem_spec),
        scratch_shapes=[
            pltpu.VMEM((row_count, width), bf16),
            pltpu.VMEM((width, units), bf16),
            pltpu.VMEM((width, units), bf16),
            pltpu.VMEM((units, width), bf16),
            pltpu.VMEM((halves, window, CAP, half), bf16),
            pltpu.VMEM((halves, ETP, window, CAP, half), bf16),
            pltpu.VMEM((halves, ETP * slots, half), bf16),
            pltpu.VMEM((ETP * slots, units), f32),
            pltpu.VMEM((ETP * slots, units), f32),
            pltpu.VMEM((ETP * slots, units), bf16),
            pltpu.VMEM((chunks, 2 * slots, piece), f32),
            pltpu.VMEM((chunks, 2 * slots, piece), bf16),
            pltpu.VMEM((chunks, 2 * slots, piece), bf16),
            pltpu.VMEM((chunks, slots, piece), bf16),
            pltpu.VMEM((chunks, slots, piece), bf16),
            pltpu.VMEM((chunks, window, CAP, piece), bf16),
            pltpu.VMEM((chunks, window, CAP, piece), bf16),
            dma((4,)),
            dma((4, halves * window)),
            dma((4, halves * window)),
            dma((chunks,)),
            dma((chunks,)),
            dma((chunks,)),
            dma((chunks,)),
            dma((chunks, window)),
            dma((chunks, window)),
        ],
        compiler_params=pltpu.CompilerParams(
            collective_id=0, has_side_effects=True, vmem_limit_bytes=56 * 1024 * 1024
        ),
    )(expert_ids.T, gate_values.T, rows_in, gate_w, up_w, down_w)
    return jnp.dot(mix, values, preferred_element_type=f32).astype(bf16)


def solution(mesh):
    in_specs = (
        P(("groups", "ep"), None),
        P(("groups", "ep"), None),
        P(("groups", "ep"), None),
        P(None, "ep"),
        P(None, "ep"),
        P("ep", None),
    )
    out_specs = P(("groups", "ep"), None)
    return jax.shard_map(body, mesh=mesh, in_specs=in_specs, out_specs=out_specs, check_vma=False)
```

```python
import functools

import jax
import jax.numpy as jnp
from jax import lax
from jax.experimental import pallas as pl
from jax.experimental.pallas import tpu as pltpu
from jax.sharding import PartitionSpec as P

ETP = 4
CAP = 8
MESH = pl.DeviceIdType.MESH


def flip(number, mask):
    result = number
    bit = 1
    while bit <= mask:
        if mask & bit:
            digit = lax.rem(lax.div(number, jnp.int32(bit)), jnp.int32(2))
            result = result + bit - 2 * bit * digit
        bit *= 2
    return result


def kernel(
    window, chunks,
    ids_ref, gates_ref, rows_hbm, gate_hbm, up_hbm, down_hbm,
    out_ref,
    rows, gate_w, up_w, down_w, block, arrived, inputs, hidden,
    own, core_out, core_in, side_out, side_in, home_out, home_in,
    load_sem, disp_send, disp_recv, core_send, core_recv, side_send, side_recv,
    home_send, home_recv,
):
    width = rows.shape[1]
    row_count = rows.shape[0]
    piece = width // chunks
    slots = window * CAP
    me = lax.axis_index("ep")
    plane = lax.div(me, jnp.int32(ETP))
    within = lax.rem(me, jnp.int32(ETP))
    sibling = plane * ETP + flip(within, 1)
    side = plane * ETP + flip(within, 2)
    partner = [flip(plane, d) * ETP + within for d in range(window)]

    loads = [
        pltpu.make_async_copy(src, dst, load_sem.at[i])
        for i, (src, dst) in enumerate(
            ((rows_hbm, rows), (gate_hbm, gate_w), (up_hbm, up_w), (down_hbm, down_w))
        )
    ]
    loads[0].start()

    barrier = pltpu.get_barrier_semaphore()
    peers = partner[1:] + [sibling, side]
    for peer in peers:
        pl.semaphore_signal(barrier, inc=1, device_id={"ep": peer}, device_id_type=MESH)

    def remote(src, dst, send, recv, target):
        return pltpu.make_async_remote_copy(
            src_ref=src, dst_ref=dst, send_sem=send, recv_sem=recv,
            device_id={"ep": target}, device_id_type=MESH,
        )

    ids = ids_ref[...]
    gates = gates_ref[...]
    named, valued = [], []
    for d in range(window):
        hit = ids == flip(plane, d)
        one = jnp.sum(jnp.where(hit, 1.0, 0.0), axis=0, keepdims=True)
        val = jnp.sum(jnp.where(hit, gates, 0.0), axis=0, keepdims=True)
        named.append(jnp.broadcast_to(one, (CAP, row_count)))
        valued.append(jnp.broadcast_to(val, (CAP, row_count)))
    named = jnp.concatenate(named, axis=0)
    valued = jnp.concatenate(valued, axis=0)
    earlier = lax.broadcasted_iota(jnp.int32, (row_count, row_count), 0) < lax.broadcasted_iota(
        jnp.int32, (row_count, row_count), 1
    )
    rank = jnp.dot(
        named.astype(jnp.bfloat16),
        jnp.where(earlier, 1.0, 0.0).astype(jnp.bfloat16),
        preferred_element_type=jnp.float32,
    )
    place = lax.rem(lax.broadcasted_iota(jnp.int32, (slots, row_count), 0), jnp.int32(CAP))
    chosen = jnp.logical_and(rank == place.astype(jnp.float32), named > 0.5)
    picker = jnp.where(chosen, 1.0, 0.0).astype(jnp.bfloat16)
    weights = jnp.where(chosen, valued, 0.0)
    high = weights.astype(jnp.bfloat16)
    low = (weights - high.astype(jnp.float32)).astype(jnp.bfloat16)
    both = jnp.concatenate([high.astype(jnp.float32), low.astype(jnp.float32)], axis=0)
    both = jnp.transpose(both).astype(jnp.bfloat16)

    loads[0].wait()
    for load in loads[1:]:
        load.start()
    for k in range(chunks):
        cols = pl.ds(k * piece, piece)
        part = jnp.dot(picker, rows[:, cols], preferred_element_type=jnp.float32)
        part = part.reshape(window, CAP, piece).astype(jnp.bfloat16)
        arrived[0, 0, :, cols] = part[0]
        for d in range(1, window):
            block[d, :, cols] = part[d]

    pl.semaphore_wait(barrier, len(peers))
    along, core, across, relay = [None], [], [], []
    for d in range(window):
        if d:
            along.append(
                remote(block.at[d], arrived.at[0, d], disp_send.at[0, d], disp_recv.at[0, d], partner[d])
            )
        core.append(
            remote(arrived.at[0, d], arrived.at[1, d], disp_send.at[1, d], disp_recv.at[1, d], sibling)
        )
        across.append(
            remote(arrived.at[0, d], arrived.at[2, d], disp_send.at[2, d], disp_recv.at[2, d], side)
        )
        relay.append(
            remote(arrived.at[2, d], arrived.at[3, d], disp_send.at[3, d], disp_recv.at[3, d], sibling)
        )
    across[0].start()
    for d in range(1, window):
        along[d].start()
    core[0].start()
    for d in range(1, window):
        along[d].wait_recv()
        across[d].start()
        core[d].start()
        across[d - 1].wait_recv()
        relay[d - 1].start()

    def gather(g):
        values = arrived[g].astype(jnp.float32).reshape(slots, width)
        inputs[g * slots:(g + 1) * slots, :] = values.astype(jnp.bfloat16)

    gather(0)
    for d in range(window):
        core[d].wait_recv()
    gather(1)
    across[window - 1].wait_recv()
    relay[window - 1].start()
    gather(2)
    for d in range(window):
        relay[d].wait_recv()
    gather(3)

    loads[1].wait()
    loads[2].wait()
    units = gate_w.shape[1]
    tile = 256

    @pl.loop(0, units // tile)
    def _(n):
        cols = pl.ds(pl.multiple_of(n * tile, tile), tile)
        g = jnp.dot(inputs[...], gate_w[:, cols], preferred_element_type=jnp.float32)
        u = jnp.dot(inputs[...], up_w[:, cols], preferred_element_type=jnp.float32)
        hidden[:, cols] = (g / (1.0 + jnp.exp(-g)) * u).astype(jnp.bfloat16)

    loads[3].wait()
    to_core = [
        remote(core_out.at[k], core_in.at[k], core_send.at[k], core_recv.at[k], sibling)
        for k in range(chunks)
    ]
    to_side = [
        remote(side_out.at[k], side_in.at[k], side_send.at[k], side_recv.at[k], side)
        for k in range(chunks)
    ]
    to_home = [
        [
            remote(home_out.at[k, d], home_in.at[k, d], home_send.at[k, d], home_recv.at[k, d], partner[d])
            for d in range(1, window)
        ]
        for k in range(chunks)
    ]

    def pair_sum(k):
        to_core[k].wait_recv()
        side_out[k] = (own[k, slots:, :] + core_in[k, slots:, :].astype(jnp.float32)).astype(jnp.bfloat16)
        to_side[k].start()
        own[k, :slots, :] = own[k, :slots, :] + core_in[k, :slots, :].astype(jnp.float32)

    def full_sum(k):
        to_side[k].wait_recv()
        total = own[k, :slots, :] + side_in[k].astype(jnp.float32)
        total = total.reshape(window, CAP, piece).astype(jnp.bfloat16)
        home_in[k, 0] = total[0]
        for d in range(1, window):
            home_out[k, d] = total[d]
        for copy in to_home[k]:
            copy.start()

    def mix(k):
        for copy in to_home[k]:
            copy.wait_recv()
        values = home_in[k].astype(jnp.float32).reshape(slots, piece)
        values = jnp.concatenate([values, values], axis=0).astype(jnp.bfloat16)
        out_ref[:, k * piece:(k + 1) * piece] = jnp.dot(
            both, values, preferred_element_type=jnp.float32
        ).astype(jnp.bfloat16)

    for k in range(chunks):
        part = jnp.dot(
            hidden[...], down_w[:, k * piece:(k + 1) * piece], preferred_element_type=jnp.float32
        )
        core_out[k, :slots, :] = part[slots:2 * slots].astype(jnp.bfloat16)
        core_out[k, slots:, :] = part[3 * slots:].astype(jnp.bfloat16)
        to_core[k].start()
        own[k, :slots, :] = part[:slots]
        own[k, slots:, :] = part[2 * slots:3 * slots]
        if k >= 1:
            pair_sum(k - 1)
    pair_sum(chunks - 1)
    for k in range(chunks):
        full_sum(k)
        if k >= 2:
            mix(k - 2)
    for k in range(max(chunks - 2, 0), chunks):
        mix(k)

    for copy in along[1:] + core + across + relay + to_core + to_side:
        copy.wait_send()
    for k in range(chunks):
        for copy in to_home[k]:
            copy.wait_send()


def body(rows_in, expert_ids, gate_values, gate_w, up_w, down_w):
    devices = lax.axis_size("ep")
    row_count, width = rows_in.shape
    units = gate_w.shape[1]
    window = devices // ETP
    slots = window * CAP
    chunks = 4
    piece = width // chunks
    bf16, f32 = jnp.bfloat16, jnp.float32
    dma = pltpu.SemaphoreType.DMA
    any_spec = pl.BlockSpec(memory_space=pl.ANY)
    vmem_spec = pl.BlockSpec(memory_space=pltpu.VMEM)
    return pl.pallas_call(
        functools.partial(kernel, window, chunks),
        out_shape=jax.ShapeDtypeStruct((row_count, width), bf16),
        in_specs=[vmem_spec, vmem_spec, any_spec, any_spec, any_spec, any_spec],
        out_specs=vmem_spec,
        scratch_shapes=[
            pltpu.VMEM((row_count, width), bf16),
            pltpu.VMEM((width, units), bf16),
            pltpu.VMEM((width, units), bf16),
            pltpu.VMEM((units, width), bf16),
            pltpu.VMEM((window, CAP, width), bf16),
            pltpu.VMEM((ETP, window, CAP, width), bf16),
            pltpu.VMEM((ETP * slots, width), bf16),
            pltpu.VMEM((ETP * slots, units), bf16),
            pltpu.VMEM((chunks, 2 * slots, piece), f32),
            pltpu.VMEM((chunks, 2 * slots, piece), bf16),
            pltpu.VMEM((chunks, 2 * slots, piece), bf16),
            pltpu.VMEM((chunks, slots, piece), bf16),
            pltpu.VMEM((chunks, slots, piece), bf16),
            pltpu.VMEM((chunks, window, CAP, piece), bf16),
            pltpu.VMEM((chunks, window, CAP, piece), bf16),
            dma((4,)),
            dma((4, window)),
            dma((4, window)),
            dma((chunks,)),
            dma((chunks,)),
            dma((chunks,)),
            dma((chunks,)),
            dma((chunks, window)),
            dma((chunks, window)),
        ],
        compiler_params=pltpu.CompilerParams(
            collective_id=0, has_side_effects=True, vmem_limit_bytes=56 * 1024 * 1024
        ),
    )(expert_ids.T, gate_values.T, rows_in, gate_w, up_w, down_w)


def solution(mesh):
    in_specs = (
        P(("groups", "ep"), None),
        P(("groups", "ep"), None),
        P(("groups", "ep"), None),
        P(None, "ep"),
        P(None, "ep"),
        P("ep", None),
    )
    out_specs = P(("groups", "ep"), None)
    return jax.shard_map(body, mesh=mesh, in_specs=in_specs, out_specs=out_specs, check_vma=False)
```

```python
import functools

import jax
import jax.numpy as jnp
from jax import lax
from jax.experimental import pallas as pl
from jax.experimental.pallas import tpu as pltpu
from jax.sharding import PartitionSpec as P

ETP = 4
CAP = 8
MESH = pl.DeviceIdType.MESH


def flip(number, mask):
    result = number
    bit = 1
    while bit <= mask:
        if mask & bit:
            digit = lax.rem(lax.div(number, jnp.int32(bit)), jnp.int32(2))
            result = result + bit - 2 * bit * digit
        bit *= 2
    return result


def kernel(
    window, chunks,
    ids_ref, gates_ref, rows_hbm, gate_hbm, up_hbm, down_hbm,
    out_hbm,
    out, rows, gate_w, up_w, down_w, block, arrived, inputs, hidden,
    own, core_out, core_in, side_out, side_in, home_out, home_in,
    load_sem, disp_send, disp_recv, core_send, core_recv, side_send, side_recv,
    home_send, home_recv, store_sem,
):
    width = rows.shape[1]
    row_count = rows.shape[0]
    piece = width // chunks
    slots = window * CAP
    me = lax.axis_index("ep")
    plane = lax.div(me, jnp.int32(ETP))
    within = lax.rem(me, jnp.int32(ETP))
    sibling = plane * ETP + flip(within, 1)
    side = plane * ETP + flip(within, 2)
    partner = [flip(plane, d) * ETP + within for d in range(window)]

    loads = [
        pltpu.make_async_copy(src, dst, load_sem.at[i])
        for i, (src, dst) in enumerate(
            ((rows_hbm, rows), (gate_hbm, gate_w), (up_hbm, up_w), (down_hbm, down_w))
        )
    ]
    loads[0].start()

    barrier = pltpu.get_barrier_semaphore()
    peers = partner[1:] + [sibling, side]
    for peer in peers:
        pl.semaphore_signal(barrier, inc=1, device_id={"ep": peer}, device_id_type=MESH)

    def remote(src, dst, send, recv, target):
        return pltpu.make_async_remote_copy(
            src_ref=src, dst_ref=dst, send_sem=send, recv_sem=recv,
            device_id={"ep": target}, device_id_type=MESH,
        )

    ids = ids_ref[...]
    gates = gates_ref[...]
    named, valued = [], []
    for d in range(window):
        hit = ids == flip(plane, d)
        one = jnp.sum(jnp.where(hit, 1.0, 0.0), axis=0, keepdims=True)
        val = jnp.sum(jnp.where(hit, gates, 0.0), axis=0, keepdims=True)
        named.append(jnp.broadcast_to(one, (CAP, row_count)))
        valued.append(jnp.broadcast_to(val, (CAP, row_count)))
    named = jnp.concatenate(named, axis=0)
    valued = jnp.concatenate(valued, axis=0)
    earlier = lax.broadcasted_iota(jnp.int32, (row_count, row_count), 0) < lax.broadcasted_iota(
        jnp.int32, (row_count, row_count), 1
    )
    rank = jnp.dot(
        named.astype(jnp.bfloat16),
        jnp.where(earlier, 1.0, 0.0).astype(jnp.bfloat16),
        preferred_element_type=jnp.float32,
    )
    place = lax.rem(lax.broadcasted_iota(jnp.int32, (slots, row_count), 0), jnp.int32(CAP))
    chosen = jnp.logical_and(rank == place.astype(jnp.float32), named > 0.5)
    picker = jnp.where(chosen, 1.0, 0.0).astype(jnp.bfloat16)
    weights = jnp.where(chosen, valued, 0.0)
    high = weights.astype(jnp.bfloat16)
    low = (weights - high.astype(jnp.float32)).astype(jnp.bfloat16)
    both = jnp.concatenate([high.astype(jnp.float32), low.astype(jnp.float32)], axis=0)
    both = jnp.transpose(both).astype(jnp.bfloat16)

    loads[0].wait()
    for load in loads[1:]:
        load.start()
    for k in range(chunks):
        cols = pl.ds(k * piece, piece)
        part = jnp.dot(picker, rows[:, cols], preferred_element_type=jnp.float32)
        part = part.reshape(window, CAP, piece).astype(jnp.bfloat16)
        arrived[0, 0, :, cols] = part[0]
        for d in range(1, window):
            block[d, :, cols] = part[d]

    pl.semaphore_wait(barrier, len(peers))
    along, core, across, relay = [None], [], [], []
    for d in range(window):
        if d:
            along.append(
                remote(block.at[d], arrived.at[0, d], disp_send.at[0, d], disp_recv.at[0, d], partner[d])
            )
        core.append(
            remote(arrived.at[0, d], arrived.at[1, d], disp_send.at[1, d], disp_recv.at[1, d], sibling)
        )
        across.append(
            remote(arrived.at[0, d], arrived.at[2, d], disp_send.at[2, d], disp_recv.at[2, d], side)
        )
        relay.append(
            remote(arrived.at[2, d], arrived.at[3, d], disp_send.at[3, d], disp_recv.at[3, d], sibling)
        )
    across[0].start()
    for d in range(1, window):
        along[d].start()
    core[0].start()
    for d in range(1, window):
        along[d].wait_recv()
        across[d].start()
        core[d].start()
        across[d - 1].wait_recv()
        relay[d - 1].start()

    def gather(g):
        values = arrived[g].astype(jnp.float32).reshape(slots, width)
        inputs[g * slots:(g + 1) * slots, :] = values.astype(jnp.bfloat16)

    gather(0)
    for d in range(window):
        core[d].wait_recv()
    gather(1)
    across[window - 1].wait_recv()
    relay[window - 1].start()
    gather(2)
    for d in range(window):
        relay[d].wait_recv()
    gather(3)

    loads[1].wait()
    loads[2].wait()
    units = gate_w.shape[1]
    tile = 256

    @pl.loop(0, units // tile)
    def _(n):
        cols = pl.ds(pl.multiple_of(n * tile, tile), tile)
        g = jnp.dot(inputs[...], gate_w[:, cols], preferred_element_type=jnp.float32)
        u = jnp.dot(inputs[...], up_w[:, cols], preferred_element_type=jnp.float32)
        hidden[:, cols] = (g / (1.0 + jnp.exp(-g)) * u).astype(jnp.bfloat16)

    loads[3].wait()
    to_core = [
        remote(core_out.at[k], core_in.at[k], core_send.at[k], core_recv.at[k], sibling)
        for k in range(chunks)
    ]
    to_side = [
        remote(side_out.at[k], side_in.at[k], side_send.at[k], side_recv.at[k], side)
        for k in range(chunks)
    ]
    to_home = [
        [
            remote(home_out.at[k, d], home_in.at[k, d], home_send.at[k, d], home_recv.at[k, d], partner[d])
            for d in range(1, window)
        ]
        for k in range(chunks)
    ]

    def pair_sum(k):
        to_core[k].wait_recv()
        side_out[k] = (own[k, slots:, :] + core_in[k, slots:, :].astype(jnp.float32)).astype(jnp.bfloat16)
        to_side[k].start()
        own[k, :slots, :] = own[k, :slots, :] + core_in[k, :slots, :].astype(jnp.float32)

    def full_sum(k):
        to_side[k].wait_recv()
        total = own[k, :slots, :] + side_in[k].astype(jnp.float32)
        total = total.reshape(window, CAP, piece).astype(jnp.bfloat16)
        home_in[k, 0] = total[0]
        for d in range(1, window):
            home_out[k, d] = total[d]
        for copy in to_home[k]:
            copy.start()

    stores = [
        pltpu.make_async_copy(out.at[k], out_hbm.at[:, pl.ds(k * piece, piece)], store_sem.at[k])
        for k in range(chunks)
    ]

    def mix(k):
        for copy in to_home[k]:
            copy.wait_recv()
        values = home_in[k].astype(jnp.float32).reshape(slots, piece)
        values = jnp.concatenate([values, values], axis=0).astype(jnp.bfloat16)
        out[k] = jnp.dot(
            both, values, preferred_element_type=jnp.float32
        ).astype(jnp.bfloat16)
        stores[k].start()

    for k in range(chunks):
        part = jnp.dot(
            hidden[...], down_w[:, k * piece:(k + 1) * piece], preferred_element_type=jnp.float32
        )
        core_out[k, :slots, :] = part[slots:2 * slots].astype(jnp.bfloat16)
        core_out[k, slots:, :] = part[3 * slots:].astype(jnp.bfloat16)
        to_core[k].start()
        own[k, :slots, :] = part[:slots]
        own[k, slots:, :] = part[2 * slots:3 * slots]
        if k >= 1:
            pair_sum(k - 1)
    pair_sum(chunks - 1)
    for k in range(chunks):
        full_sum(k)
        if k >= 2:
            mix(k - 2)
    for k in range(max(chunks - 2, 0), chunks):
        mix(k)

    for copy in along[1:] + core + across + relay + to_core + to_side:
        copy.wait_send()
    for k in range(chunks):
        for copy in to_home[k]:
            copy.wait_send()
        stores[k].wait()


def body(rows_in, expert_ids, gate_values, gate_w, up_w, down_w):
    devices = lax.axis_size("ep")
    row_count, width = rows_in.shape
    units = gate_w.shape[1]
    window = devices // ETP
    slots = window * CAP
    chunks = 4
    piece = width // chunks
    bf16, f32 = jnp.bfloat16, jnp.float32
    dma = pltpu.SemaphoreType.DMA
    any_spec = pl.BlockSpec(memory_space=pl.ANY)
    vmem_spec = pl.BlockSpec(memory_space=pltpu.VMEM)
    return pl.pallas_call(
        functools.partial(kernel, window, chunks),
        out_shape=jax.ShapeDtypeStruct((row_count, width), bf16),
        in_specs=[vmem_spec, vmem_spec, any_spec, any_spec, any_spec, any_spec],
        out_specs=any_spec,
        scratch_shapes=[
            pltpu.VMEM((chunks, row_count, piece), bf16),
            pltpu.VMEM((row_count, width), bf16),
            pltpu.VMEM((width, units), bf16),
            pltpu.VMEM((width, units), bf16),
            pltpu.VMEM((units, width), bf16),
            pltpu.VMEM((window, CAP, width), bf16),
            pltpu.VMEM((ETP, window, CAP, width), bf16),
            pltpu.VMEM((ETP * slots, width), bf16),
            pltpu.VMEM((ETP * slots, units), bf16),
            pltpu.VMEM((chunks, 2 * slots, piece), f32),
            pltpu.VMEM((chunks, 2 * slots, piece), bf16),
            pltpu.VMEM((chunks, 2 * slots, piece), bf16),
            pltpu.VMEM((chunks, slots, piece), bf16),
            pltpu.VMEM((chunks, slots, piece), bf16),
            pltpu.VMEM((chunks, window, CAP, piece), bf16),
            pltpu.VMEM((chunks, window, CAP, piece), bf16),
            dma((4,)),
            dma((4, window)),
            dma((4, window)),
            dma((chunks,)),
            dma((chunks,)),
            dma((chunks,)),
            dma((chunks,)),
            dma((chunks, window)),
            dma((chunks, window)),
            dma((chunks,)),
        ],
        compiler_params=pltpu.CompilerParams(
            collective_id=0, has_side_effects=True, vmem_limit_bytes=56 * 1024 * 1024
        ),
    )(expert_ids.T, gate_values.T, rows_in, gate_w, up_w, down_w)


def solution(mesh):
    in_specs = (
        P(("groups", "ep"), None),
        P(("groups", "ep"), None),
        P(("groups", "ep"), None),
        P(None, "ep"),
        P(None, "ep"),
        P("ep", None),
    )
    out_specs = P(("groups", "ep"), None)
    return jax.shard_map(body, mesh=mesh, in_specs=in_specs, out_specs=out_specs, check_vma=False)
```
